256 devices in a mesh: row: 16 (over z_lo, x), col: 16 (over z_hi, y, core).
Axes of the slice: x: 4, y: 4, z: 8 (z_hi: 2, z_lo: 4; z = z_hi * 4 + z_lo), core: 2. Of those that a mesh axis runs over, the one named last changes fastest.
Arguments:
- leaf_multipoles: float32 [121, 64, 64, 48], P(None, 'row', 'col'), may hold values from -6 to 6
- occupancy: int32 [64, 64, 48], P('row', 'col'), may hold values 0 or 1
- m2m_ops: bfloat16 [2, 2, 2, 121, 121], replicated, may hold values from -0.1875 to 0.1875
- m2l_ops: bfloat16 [7, 7, 7, 121, 121], replicated, may hold values from -0.078125 to 0.078125
- l2l_ops: bfloat16 [2, 2, 2, 121, 121], replicated, may hold values from -0.375 to 0.375
Outputs:
- local_expansions: float32 [121, 64, 64, 48], P(None, 'row', 'col')
The draws below stay inside these ranges and needn't reach their ends.
All inputs are finite; a program needn't handle non-finite values. No bound on the sum of `occupancy` on one device may be relied on, other than what follows from the above.
Results may differ from the reference program's by a relative error of at most 0.006.
Values may be sent and summed in bfloat16 or wider, within the bound.
A program may use at most 128 MiB of HBM per device.

```python
import jax
import jax.numpy as jnp
from jax import lax

C = 121
BZ = 48
NX = 64
NY = 64


def set_ends(result, stream_key, low, largest):
    place = [jax.random.randint(jax.random.fold_in(stream_key, axis), (), 0, length) for axis, length in enumerate(result.shape)]
    longest = result.shape.index(max(result.shape))
    beside = place[:longest] + [(place[longest] + 1) % result.shape[longest]] + place[longest + 1:]
    return result.at[tuple(place)].set(low).at[tuple(beside)].set(largest)


def shard_levels(own_key, extent, pieces, low, high):
    level = 1.0
    for axis_at, parts in pieces:
        draws = jax.random.uniform(jax.random.fold_in(jax.random.fold_in(own_key, 6), axis_at), (parts,), jnp.float32, low / len(pieces), high / len(pieces))
        level = level * jnp.repeat(jnp.exp(draws), extent[axis_at] // parts).reshape((-1,) + (1,) * (len(extent) - 1 - axis_at))
    return level


def gaussian(stream_key, dims, width, reach, pieces=(), kind=jnp.bfloat16):
    entries = width * jax.random.normal(stream_key, dims, jnp.float32)
    if pieces:
        entries = entries * shard_levels(stream_key, dims, pieces, -0.22, 0.18)
    return jnp.clip(entries, -reach, reach).astype(kind)


def setup_inputs(seed: int = 0) -> dict:
    splits = jax.random.split(jax.random.key(seed), 6)
    leaf_multipoles = gaussian(splits[0], (C, NX, NY, BZ), 1.0, 6.0, ((1, 16), (2, 16)), jnp.float32)
    occupancy = set_ends((jax.random.randint(splits[1], (NX, NY, BZ), 0, 4) < 3).astype(jnp.int32), jax.random.fold_in(splits[1], 1), 0, 1)
    m2m_ops = gaussian(splits[2], (2, 2, 2, C, C), (8 * C) ** -0.5, 0.1875)
    m2l_ops = gaussian(splits[3], (7, 7, 7, C, C), (48 * C) ** -0.5, 0.078125)
    l2l_ops = gaussian(splits[4], (2, 2, 2, C, C), (2 * C) ** -0.5, 0.375)
    return dict(leaf_multipoles=leaf_multipoles, occupancy=occupancy, m2m_ops=m2m_ops, m2l_ops=m2l_ops, l2l_ops=l2l_ops)


def keep_offsets():
    offsets_axis = jnp.arange(7) - 3
    near_axis = jnp.abs(offsets_axis) <= 1
    central = near_axis[:, None, None] & near_axis[None, :, None] & near_axis[None, None, :]
    return jnp.where(central, 0.0, 1.0)[:, :, :, None, None]


def pad_window(cells):
    return jnp.pad(cells, ((0, 0), (3, 3 + cells.shape[1] % 2), (3, 3 + cells.shape[2] % 2), (3, 3 + cells.shape[3] % 2)))


def expand(padded):
    channels = padded.shape[0]
    half_x = (padded.shape[1] - 6) // 2
    half_y = (padded.shape[2] - 6) // 2
    half_z = (padded.shape[3] - 6) // 2
    central = padded[:, 1:2 * half_x + 5, 1:2 * half_y + 5, 1:2 * half_z + 5]
    central = central.reshape(channels, half_x + 2, 2, half_y + 2, 2, half_z + 2, 2)
    central = jnp.stack([central[:, shift_x:shift_x + half_x] for shift_x in range(3)], 0)
    central = jnp.stack([central[:, :, :, :, shift_y:shift_y + half_y] for shift_y in range(3)], 0)
    central = jnp.stack([central[:, :, :, :, :, :, :, shift_z:shift_z + half_z] for shift_z in range(3)], 0)
    central = jnp.transpose(central, (2, 5, 1, 7, 0, 9, 3, 4, 6, 8))
    return central.reshape(6, 6, 6, channels, half_x * half_y * half_z)


def alternate(parity_parts, half_x, half_y, half_z):
    channels = parity_parts.shape[3]
    cells = parity_parts.reshape(2, 2, 2, channels, half_x, half_y, half_z)
    cells = jnp.transpose(cells, (3, 4, 0, 5, 1, 6, 2))
    return cells.reshape(channels, 2 * half_x, 2 * half_y, 2 * half_z)


def upward(children, m2m_wide):
    blocks = children.astype(jnp.float32).reshape(children.shape[0], children.shape[1] // 2, 2, children.shape[2] // 2, 2, children.shape[3] // 2, 2)
    return jnp.einsum("abcoi,ixaybzc->oxyz", m2m_wide, blocks, precision=lax.Precision.HIGHEST)


def downward(parents, l2l_wide):
    children = jnp.einsum("abcoi,ixyz->oxaybzc", l2l_wide, parents.astype(jnp.float32), precision=lax.Precision.HIGHEST)
    return children.reshape(children.shape[0], 2 * children.shape[1], 2 * children.shape[3], 2 * children.shape[5])


def translate_level(cells, m2l_wide):
    channels = cells.shape[0]
    padded = pad_window(cells)
    half_y = (padded.shape[2] - 6) // 2
    half_z = (padded.shape[3] - 6) // 2
    width_x = padded.shape[1] - 6
    slab_width = min(width_x, 8)

    def one_block(number):
        window = lax.dynamic_slice_in_dim(padded, (number * slab_width).astype(jnp.int32), slab_width + 6, 1)
        spread = expand(window).astype(jnp.float32)
        results = []
        for parity_x in range(2):
            for parity_y in range(2):
                for parity_z in range(2):
                    operator_block = m2l_wide[1 - parity_x:7 - parity_x, 1 - parity_y:7 - parity_y, 1 - parity_z:7 - parity_z]
                    results.append(jnp.einsum("xyzoi,xyzit->ot", operator_block, spread, precision=lax.Precision.HIGHEST))
        parity_parts = jnp.stack(results, 0).reshape(2, 2, 2, channels, spread.shape[4])
        return alternate(parity_parts, slab_width // 2, half_y, half_z)

    blocks = lax.map(one_block, jnp.arange(width_x // slab_width, dtype=jnp.int32))
    result_field = jnp.transpose(blocks, (1, 0, 2, 3, 4)).reshape(channels, width_x, 2 * half_y, 2 * half_z)
    return result_field[:, :cells.shape[1], :cells.shape[2], :cells.shape[3]]


def reference(leaf_multipoles, occupancy, m2m_ops, m2l_ops, l2l_ops):
    m2m_wide = m2m_ops.astype(jnp.float32)
    l2l_wide = l2l_ops.astype(jnp.float32)
    m2l_wide = m2l_ops.astype(jnp.float32) * keep_offsets().astype(jnp.float32)
    leaves = (leaf_multipoles * occupancy.astype(jnp.float32)).astype(jnp.bfloat16)
    levels = [leaves]
    for repeat in range(4):
        levels.append(upward(levels[-1], m2m_wide).astype(jnp.bfloat16))
    local_field = translate_level(levels[4], m2l_wide)
    for finer in (3, 2, 1, 0):
        local_field = downward(local_field.astype(jnp.bfloat16), l2l_wide) + translate_level(levels[finer], m2l_wide)
    return local_field
```

```python
import functools

import jax
import jax.numpy as jnp
from jax import lax
from jax.experimental import pallas as pl
from jax.experimental.pallas import tpu as pltpu
from jax.sharding import PartitionSpec as P

MESH = pl.DeviceIdType.MESH
C = 121
F32 = jnp.float32
BF16 = jnp.bfloat16
AROUND = [(dr, dc) for dr in (-1, 0, 1) for dc in (-1, 0, 1) if (dr, dc) != (0, 0)]
MATES = [(0, 1), (1, 0), (1, 1)]


def dot(x, w):
    return jnp.dot(x, w, preferred_element_type=F32)


def swap(v):
    return 2 * (v % 2) + v // 2


def kernel(
    leaf, occ, wm, wl, ops_hbm,
    out,
    ops, opt, s6, w6, n5, w5, w4, n4, t3, m3, n3, n2, nat, col, t6, ts, f6, fs, ls,
    ops_sem, s6_send, s6_recv, s5_send, s5_recv, a_send, a_recv, b_send, b_recv,
    c_send, c_recv, d_send, d_recv,
):
    r, c = lax.axis_index("row"), lax.axis_index("col")
    nr, nc = lax.axis_size("row"), lax.axis_size("col")

    ops_copies = [
        pltpu.make_async_copy(ops_hbm.at[dx], ops.at[dx], ops_sem.at[dx]) for dx in range(7)
    ]
    for copy in ops_copies:
        copy.start()

    def inside(rr, cc):
        return (rr >= 0) & (rr < nr) & (cc >= 0) & (cc < nc)

    def partner(n):
        return 4 * (n // 4) + swap(r % 4), 4 * (n % 4) + swap(c % 4)

    barrier = pltpu.get_barrier_semaphore()
    greeted = jnp.int32(0)
    for scale in (1, 2):
        for dr, dc in AROUND:
            rr, cc = r + scale * dr, c + scale * dc
            there = inside(rr, cc)

            @pl.when(there)
            def _():
                pl.semaphore_signal(
                    barrier, inc=1, device_id={"row": rr, "col": cc}, device_id_type=MESH
                )

            greeted = greeted + there.astype(jnp.int32)
    for n in range(16):
        rr, cc = partner(n)
        other = (rr != r) | (cc != c)

        @pl.when(other)
        def _():
            pl.semaphore_signal(
                barrier, inc=1, device_id={"row": rr, "col": cc}, device_id_type=MESH
            )

        greeted = greeted + other.astype(jnp.int32)

    s6[...] = jnp.zeros_like(s6)
    occ_t = jnp.transpose(
        jnp.concatenate([occ[x].astype(F32) for x in range(4)], axis=0)
    )
    for x in range(4):
        for y in range(4):
            here = 4 * x + y
            s6[x, y, :, 0:C] = leaf[x, y] * occ_t[:, here : here + 1]
    for x in range(2):
        for y in range(4):
            for a in range(2):
                w6[1 + x, 2 + y, :, a * 128 : (a + 1) * 128] = s6[2 * x + a, y].astype(BF16)

    total = jnp.zeros((96, 128), F32)
    for b in range(2):
        for cz in range(2):
            rows = []
            for x in range(2):
                for y in range(2):
                    rows.append(
                        jnp.concatenate(
                            [s6[2 * x + a, 2 * y + b, pl.ds(cz, 24, stride=2), :] for a in range(2)],
                            axis=1,
                        )
                    )
            total = total + dot(jnp.concatenate(rows, axis=0).astype(BF16), wm[2 * b + cz])
    n5[:, 48:64, :] = jnp.zeros((2, 16, 128), F32)
    for x in range(2):
        n5[x, 0:48, :] = total[48 * x : 48 * x + 48]
        w5[1, 1, :, 128 * x : 128 * x + 128] = total[48 * x : 48 * x + 48].astype(BF16)

    total = jnp.zeros((16, 128), F32)
    for b in range(2):
        for cz in range(2):
            rows = jnp.concatenate(
                [n5[a, pl.ds(24 * b + cz, 16, stride=2), :] for a in range(2)], axis=1
            )
            total = total + dot(rows.astype(BF16), wm[2 * b + cz])
    depth = lax.broadcasted_iota(jnp.int32, (16, 128), 0)
    w4[1, 1, r % 2, c % 2] = jnp.where(depth < 12, total, 0.0).astype(BF16)

    @pl.when(r == 0)
    def _():
        w6[0] = jnp.zeros_like(w6[0])
        w5[0] = jnp.zeros_like(w5[0])

    @pl.when(r == nr - 1)
    def _():
        w6[3] = jnp.zeros_like(w6[3])
        w5[2] = jnp.zeros_like(w5[2])

    @pl.when(c == 0)
    def _():
        w6[:, 0:2] = jnp.zeros_like(w6[:, 0:2])
        w5[:, 0] = jnp.zeros_like(w5[:, 0])

    @pl.when(c == nc - 1)
    def _():
        w6[:, 6:8] = jnp.zeros_like(w6[:, 6:8])
        w5[:, 2] = jnp.zeros_like(w5[:, 2])

    @pl.when(r // 2 == 0)
    def _():
        w4[0] = jnp.zeros_like(w4[0])

    @pl.when(r // 2 == nr // 2 - 1)
    def _():
        w4[2] = jnp.zeros_like(w4[2])

    @pl.when(c // 2 == 0)
    def _():
        w4[:, 0] = jnp.zeros_like(w4[:, 0])

    @pl.when(c // 2 == nc // 2 - 1)
    def _():
        w4[:, 2] = jnp.zeros_like(w4[:, 2])

    pl.semaphore_wait(barrier, greeted)

    def remote(src, dst, send, recv, rr, cc):
        return pltpu.make_async_remote_copy(
            src_ref=src,
            dst_ref=dst,
            send_sem=send,
            recv_sem=recv,
            device_id={"row": rr, "col": cc},
            device_id_type=MESH,
        )

    def mate_copy(n):
        dr, dc = MATES[n]
        tile = w4.at[1, 1, r % 2, c % 2]
        return remote(
            tile, tile, a_send.at[n], a_recv.at[n], r + dr * (1 - 2 * (r % 2)), c + dc * (1 - 2 * (c % 2))
        )

    def mate_landing(n):
        dr, dc = MATES[n]
        tile = w4.at[1, 1, (r + dr) % 2, (c + dc) % 2]
        return remote(tile, tile, a_send.at[n], a_recv.at[n], r, c)

    def span(d, own, low, high, width):
        if d == 0:
            return pl.ds(own, 2 * width), pl.ds(own, 2 * width)
        if d < 0:
            return pl.ds(own, width), pl.ds(high, width)
        return pl.ds(own + width, width), pl.ds(low, width)

    def rim_copy(n):
        dr, dc = AROUND[n]
        sx, tx = span(dr, 1, 0, 3, 1)
        sy, ty = span(dc, 2, 0, 6, 2)
        return remote(
            w6.at[sx, sy], w6.at[tx, ty], s6_send.at[n], s6_recv.at[n], r + dr, c + dc
        )

    def five_copy(n):
        dr, dc = AROUND[n]
        return remote(
            w5.at[1, 1], w5.at[1 - dr, 1 - dc], s5_send.at[n], s5_recv.at[n], r + dr, c + dc
        )

    def four_copy(n):
        dr, dc = AROUND[n]
        return remote(
            w4.at[1, 1], w4.at[1 - dr, 1 - dc], b_send.at[n], b_recv.at[n], r + 2 * dr, c + 2 * dc
        )

    def sends_to(n, scale):
        dr, dc = AROUND[n]
        return inside(r + scale * dr, c + scale * dc)

    def gets_from(n, scale):
        dr, dc = AROUND[n]
        return inside(r - scale * dr, c - scale * dc)

    def each(make, scale, wanted, act):
        for n in range(8):

            @pl.when(wanted(n, scale))
            def _():
                act(make(n))

    for n in range(3):
        mate_copy(n).start()
    each(five_copy, 1, sends_to, lambda copy: copy.start())
    each(rim_copy, 1, sends_to, lambda copy: copy.start())

    opt_pad = jnp.zeros((7, 128), BF16)
    opt_side = jnp.zeros((128, 7), BF16)

    def turn(dx):
        ops_copies[dx].wait()

        def one(n, _):
            dy, dz = n // 7, n % 7
            block = jnp.concatenate(
                [jnp.concatenate([ops[dx, dy, dz], opt_pad[:, 0:C]], axis=0), opt_side], axis=1
            )
            opt[dx, dy, dz] = jnp.transpose(block)
            return 0

        lax.fori_loop(0, 49, one, 0)
        if 2 <= dx <= 4:
            for dy in range(2, 5):
                for dz in range(2, 5):
                    opt[dx, dy, dz] = jnp.zeros((128, 128), BF16)

    for dx in (0, 1):
        turn(dx)

    for n in range(3):
        mate_landing(n).wait_recv()
    for b in range(2):
        for a in range(2):
            n4[b, a] = w4[1, 1, a, b].astype(F32)
    total = jnp.zeros((16, 128), F32)
    for b in range(2):
        for cz in range(2):
            rows = jnp.concatenate(
                [
                    jnp.concatenate([n4[b, a, pl.ds(cz, 8, stride=2), :] for a in range(2)], axis=1),
                    jnp.zeros((8, 256), F32),
                ],
                axis=0,
            )
            total = total + dot(rows.astype(BF16), wm[2 * b + cz])
    t3[...] = jnp.where(depth < 6, total, 0.0).astype(BF16)

    def three_copy(n):
        rr, cc = partner(n)
        return remote(
            t3,
            m3.at[(r // 2) % 2, (c // 2) % 2, r // 4, c // 4],
            c_send.at[n],
            c_recv.at[4 * (r // 4) + c // 4],
            rr,
            cc,
        )

    def three_landing(n):
        return remote(t3, m3.at[r % 2, c % 2, n // 4, n % 4], c_send.at[n], c_recv.at[n], r, c)

    def is_other(n):
        rr, cc = partner(n)
        return (rr != r) | (cc != c)

    def over_partners(act):
        def step(n, _):
            @pl.when(is_other(n))
            def _():
                act(n)

            return 0

        lax.fori_loop(0, 16, step, 0)

    over_partners(lambda n: three_copy(n).start())

    @pl.when((swap(r % 4) == r % 4) & (swap(c % 4) == c % 4))
    def _():
        m3[r % 2, c % 2, r // 4, c // 4] = t3[...]

    each(four_copy, 2, sends_to, lambda copy: copy.start())

    for dx in (2, 3, 4):
        turn(dx)

    over_partners(lambda n: three_landing(n).wait_recv())

    def share_copy(n):
        dr, dc = MATES[n]
        part = m3.at[r % 2, c % 2]
        return remote(
            part, part, d_send.at[n], d_recv.at[n], r + dr * (1 - 2 * (r % 2)), c + dc * (1 - 2 * (c % 2))
        )

    def share_landing(n):
        dr, dc = MATES[n]
        part = m3.at[(r + dr) % 2, (c + dc) % 2]
        return remote(part, part, d_send.at[n], d_recv.at[n], r, c)

    for n in range(3):
        share_copy(n).start()
    for dx in (5, 6):
        turn(dx)
    for n in range(3):
        share_landing(n).wait_recv()

    for b in range(2):
        for i in range(4):
            for a in range(2):
                n3[b, a, 64 * i : 64 * i + 64] = jnp.concatenate(
                    [m3[a, b, i, j].astype(F32) for j in range(4)], axis=0
                )
    total = jnp.zeros((128, 128), F32)
    for b in range(2):
        for cz in range(2):
            rows = jnp.concatenate(
                [n3[b, a, pl.ds(cz, 128, stride=2), :] for a in range(2)], axis=1
            )
            total = total + dot(rows.astype(BF16), wm[2 * b + cz])
    for n in range(16):
        n2[n // 4, n % 4] = total[8 * n : 8 * n + 8]

    each(four_copy, 2, gets_from, lambda copy: copy.wait_recv())
    each(five_copy, 1, gets_from, lambda copy: copy.wait_recv())
    row8 = lax.broadcasted_iota(jnp.int32, (8, 256), 0)
    from_below = (row8 == 1) | (row8 == 2) | (row8 == 3) | (row8 == 5)
    from_above = (row8 == 0) | (row8 == 1) | (row8 == 2) | (row8 == 4)

    def wide(ref, k):
        return jnp.concatenate([ref[a, pl.ds(k, 8, stride=6), :] for a in range(2)], axis=1)

    def levels(column, below, above):
        v = [column(k) for k in range(6)]
        low = [jnp.where(below, pltpu.roll(v[k], 1, axis=0), 0.0) for k in (4, 5)]
        high = [jnp.where(above, pltpu.roll(v[k], 7, axis=0), 0.0) for k in (0, 1)]
        return low + v + high

    def coarse(n, _):
        x, y = n // 6, n % 6
        half, odd = y // 2, y % 2
        five = w5[x, half].astype(F32)
        five = jnp.where(odd == 0, five[0:24], five[24:48])
        i3, j3 = r // 4 - 1 + x, c // 4 - 1 + half
        ok3 = (i3 >= 0) & (i3 < 4) & (j3 >= 0) & (j3 < 4)
        j2 = 2 * (c // 8) - 2 + y
        for a in range(2):
            nat[a, 0:24] = five[:, 128 * a : 128 * a + 128]
            nat[a, 24:36] = w4[x, half, a, odd].astype(F32)[0:12]
            three = m3[a, odd, jnp.clip(i3, 0, 3), jnp.clip(j3, 0, 3)].astype(F32)
            nat[a, 36:42] = jnp.where(ok3, three[0:6], 0.0)
            i2 = 2 * (r // 8 - 1 + x) + a
            ok2 = (i2 >= 0) & (i2 < 4) & (j2 >= 0) & (j2 < 4)
            two = n2[jnp.clip(i2, 0, 3), jnp.clip(j2, 0, 3)]
            nat[a, 42:48] = jnp.where(ok2, two[0:6], 0.0)
        v = levels(lambda k: wide(nat, k), from_below, from_above)
        for s in range(6):
            ts[x, y, s] = jnp.concatenate(
                [v[s], v[s + 2], v[s + 4], jnp.zeros((8, 256), F32)], axis=0
            ).astype(BF16)
        return 0

    lax.fori_loop(0, 18, coarse, 0)

    each(rim_copy, 1, gets_from, lambda copy: copy.wait_recv())

    def fine(y, _):
        before = None
        for x in range(4):
            whole = w6[x, y].astype(F32)
            for a in range(2):
                col[x, a] = whole[:, 128 * a : 128 * a + 128]
            v = levels(lambda k: wide(col.at[x], k), row8 >= 1, row8 <= 6)
            if before is not None:
                for k in range(10):
                    t6[x - 1, y, k] = jnp.concatenate([before[k], v[k]], axis=0).astype(BF16)
            before = v
        return 0

    lax.fori_loop(0, 8, fine, 0)

    def far(p, _):
        py, pz = p // 2, p % 2
        near = [-1, 0, 1, -2, 2]
        total = jnp.zeros((128, 256), F32)
        for j in range(3):
            for ey in range(6):
                dy = near[ey] if ey < 5 else 3 - 6 * py
                for ez in range(6):
                    dz = near[ez] if ez < 5 else 3 - 6 * pz
                    if j == 1 and ey < 3 and ez < 3:
                        continue
                    y0, k0 = py + dy + 2, pz + dz + 2
                    x = jnp.concatenate(
                        [t6[j, y0 + 2 * t, k0 + 2 * m] for t in range(2) for m in range(3)]
                        + [ts[j, y0, k0]],
                        axis=0,
                    )
                    w = jnp.concatenate(
                        [
                            jnp.concatenate(
                                [opt[2 * j + a - 2 - px + 3, dy + 3, dz + 3] for px in range(2)],
                                axis=1,
                            )
                            for a in range(2)
                        ],
                        axis=0,
                    )
                    total = total + dot(x, w)
        for px in range(2):
            lanes = slice(128 * px, 128 * px + 128)
            for m in range(3):
                zs = pl.ds(2 * m + pz, 8, stride=6)
                for t in range(2):
                    for g in range(2):
                        at = 48 * t + 16 * m + 8 * g
                        f6[2 * g + px, py + 2 * t, zs, :] = total[at : at + 8, lanes]
                fs[px, py, zs, :] = total[96 + 8 * m : 104 + 8 * m, lanes]
        return 0

    lax.fori_loop(0, 4, far, 0)

    def refine(parents, a, b):
        return dot(parents.astype(BF16), wl[2 * a + b])

    ls[...] = jnp.zeros_like(ls)
    two = fs[(r // 4) % 2, (c // 4) % 2, 40:48, :]
    ls[0, 0:8] = two
    two = jnp.concatenate([ls[0, 2:8], jnp.zeros((10, 128), F32)], axis=0)
    both = refine(two, (r // 2) % 2, (c // 2) % 2)
    for cz in range(2):
        ls[1, pl.ds(cz, 8, stride=2), :] = both[0:8, 128 * cz : 128 * cz + 128]
    three = ls[1, 0:6] + fs[(r // 2) % 2, (c // 2) % 2, 36:42, :]
    three = jnp.concatenate([three, jnp.zeros((10, 128), F32)], axis=0)
    both = refine(three, r % 2, c % 2)
    for cz in range(2):
        ls[2, pl.ds(cz, 8, stride=2), :] = both[0:8, 128 * cz : 128 * cz + 128]
    four = ls[2, 0:12] + fs[r % 2, c % 2, 24:36, :]
    four = jnp.concatenate([four, jnp.zeros((4, 128), F32)], axis=0)
    fives = []
    for a in range(2):
        for b in range(2):
            both = refine(four, a, b)
            for cz in range(2):
                ls[3 + 2 * a + b, pl.ds(cz, 16, stride=2), :] = both[:, 128 * cz : 128 * cz + 128]
            fives.append(ls[3 + 2 * a + b, 0:24] + fs[a, b, 0:24, :])
    five = jnp.concatenate(fives, axis=0).astype(BF16)
    for a in range(2):
        for b in range(2):
            both = dot(five, wl[2 * a + b])
            for x in range(2):
                for y in range(2):
                    at = 24 * (2 * x + y)
                    for cz in range(2):
                        zs = pl.ds(cz, 24, stride=2)
                        s6[2 * x + a, 2 * y + b, zs, :] = (
                            f6[2 * x + a, 2 * y + b, zs, :]
                            + both[at : at + 24, 128 * cz : 128 * cz + 128]
                        )
    out[...] = s6[:, :, :, 0:C]

    for n in range(3):
        mate_copy(n).wait_send()
        share_copy(n).wait_send()
    each(five_copy, 1, sends_to, lambda copy: copy.wait_send())
    each(rim_copy, 1, sends_to, lambda copy: copy.wait_send())
    each(four_copy, 2, sends_to, lambda copy: copy.wait_send())
    over_partners(lambda n: three_copy(n).wait_send())


def local(leaf_multipoles, occupancy, m2m_ops, m2l_ops, l2l_ops):
    leaf = jnp.transpose(leaf_multipoles, (1, 2, 3, 0))
    pad = 128 - C
    wm = jnp.pad(
        jnp.transpose(m2m_ops, (1, 2, 0, 4, 3)), ((0, 0),) * 3 + ((0, pad), (0, pad))
    ).reshape(4, 256, 128)
    wl = jnp.pad(
        jnp.transpose(l2l_ops, (0, 1, 4, 2, 3)), ((0, 0),) * 2 + ((0, pad), (0, 0), (0, pad))
    ).reshape(4, 128, 256)
    vmem = pl.BlockSpec(memory_space=pltpu.VMEM)
    dma = pltpu.SemaphoreType.DMA
    result = pl.pallas_call(
        kernel,
        out_shape=jax.ShapeDtypeStruct((4, 4, 48, C), F32),
        in_specs=[vmem] * 4 + [pl.BlockSpec(memory_space=pl.ANY)],
        out_specs=vmem,
        scratch_shapes=[
            pltpu.VMEM((7, 7, 7, C, C), BF16),
            pltpu.VMEM((7, 7, 7, 128, 128), BF16),
            pltpu.VMEM((4, 4, 48, 128), F32),
            pltpu.VMEM((4, 8, 48, 256), BF16),
            pltpu.VMEM((2, 64, 128), F32),
            pltpu.VMEM((3, 3, 48, 256), BF16),
            pltpu.VMEM((3, 3, 2, 2, 16, 128), BF16),
            pltpu.VMEM((2, 2, 16, 128), F32),
            pltpu.VMEM((16, 128), BF16),
            pltpu.VMEM((2, 2, 4, 4, 16, 128), BF16),
            pltpu.VMEM((2, 2, 256, 128), F32),
            pltpu.VMEM((4, 4, 8, 128), F32),
            pltpu.VMEM((2, 48, 128), F32),
            pltpu.VMEM((4, 2, 48, 128), F32),
            pltpu.VMEM((3, 8, 10, 16, 256), BF16),
            pltpu.VMEM((3, 6, 6, 32, 256), BF16),
            pltpu.VMEM((4, 4, 48, 128), F32),
            pltpu.VMEM((2, 2, 48, 128), F32),
            pltpu.VMEM((7, 32, 128), F32),
            dma((7,)),
            dma((8,)),
            dma((8,)),
            dma((8,)),
            dma((8,)),
            dma((3,)),
            dma((3,)),
            dma((8,)),
            dma((8,)),
            dma((16,)),
            dma((16,)),
            dma((3,)),
            dma((3,)),
        ],
        compiler_params=pltpu.CompilerParams(
            collective_id=0, has_side_effects=True, vmem_limit_bytes=56 * 2**20
        ),
    )(leaf, occupancy, wm, wl, m2l_ops)
    return jnp.transpose(result, (3, 0, 1, 2))


def solution(mesh):
    placed = (P(None, "row", "col", None), P("row", "col", None), P(), P(), P())
    return jax.shard_map(
        local, mesh=mesh, in_specs=placed, out_specs=P(None, "row", "col", None), check_vma=False
    )
```

```python
import functools

import jax
import jax.numpy as jnp
from jax import lax
from jax.experimental import pallas as pl
from jax.experimental.pallas import tpu as pltpu
from jax.sharding import PartitionSpec as P

MESH = pl.DeviceIdType.MESH
C = 121
F32 = jnp.float32
BF16 = jnp.bfloat16
AROUND = [(dr, dc) for dr in (-1, 0, 1) for dc in (-1, 0, 1) if (dr, dc) != (0, 0)]
MATES = [(0, 1), (1, 0), (1, 1)]


def dot(x, w):
    return jnp.dot(x, w, preferred_element_type=F32)


def swap(v):
    return 2 * (v % 2) + v // 2


def kernel(
    leaf, occ, m2m, l2l, ops_hbm,
    out,
    ops, opt, mf, wm, lf, wl, s6, w6, n5, w5, w4, n4, t3, m3, n3, n2, nat, col, t6, ts, f6, fs, ls,
    ops_sem, s6_send, s6_recv, s5_send, s5_recv, a_send, a_recv, b_send, b_recv,
    c_send, c_recv, d_send, d_recv,
):
    r, c = lax.axis_index("row"), lax.axis_index("col")
    nr, nc = lax.axis_size("row"), lax.axis_size("col")

    ops_copies = [
        pltpu.make_async_copy(ops_hbm.at[dx], ops.at[dx], ops_sem.at[dx]) for dx in range(7)
    ]
    for copy in ops_copies:
        copy.start()

    def inside(rr, cc):
        return (rr >= 0) & (rr < nr) & (cc >= 0) & (cc < nc)

    def partner(n):
        return 4 * (n // 4) + swap(r % 4), 4 * (n % 4) + swap(c % 4)

    barrier = pltpu.get_barrier_semaphore()
    greeted = jnp.int32(0)
    for scale in (1, 2):
        for dr, dc in AROUND:
            rr, cc = r + scale * dr, c + scale * dc
            there = inside(rr, cc)

            @pl.when(there)
            def _():
                pl.semaphore_signal(
                    barrier, inc=1, device_id={"row": rr, "col": cc}, device_id_type=MESH
                )

            greeted = greeted + there.astype(jnp.int32)
    for n in range(16):
        rr, cc = partner(n)
        other = (rr != r) | (cc != c)

        @pl.when(other)
        def _():
            pl.semaphore_signal(
                barrier, inc=1, device_id={"row": rr, "col": cc}, device_id_type=MESH
            )

        greeted = greeted + other.astype(jnp.int32)

    s6[...] = jnp.zeros_like(s6)
    occ_t = jnp.transpose(
        jnp.concatenate([occ[x].astype(F32) for x in range(4)], axis=0)
    )
    for x in range(4):
        for y in range(4):
            here = 4 * x + y
            s6[x, y, :, 0:C] = leaf[x, y] * occ_t[:, here : here + 1]
    for x in range(2):
        for y in range(4):
            for a in range(2):
                w6[1 + x, 2 + y, :, a * 128 : (a + 1) * 128] = s6[2 * x + a, y].astype(BF16)

    def octant(raw, a, b, cz):
        rows = raw[pl.ds((2 * a + b) * 2 * C + cz, 128, stride=2), :]
        return jnp.transpose(rows)[0:C, 0:C].astype(BF16)

    mf[0 : 8 * C, 0:C] = m2m[...].astype(F32)
    wm[...] = jnp.zeros_like(wm)
    for a in range(2):
        for b in range(2):
            for cz in range(2):
                wm[2 * b + cz, 128 * a : 128 * a + C, 0:C] = octant(mf, a, b, cz)

    total = jnp.zeros((96, 128), F32)
    for b in range(2):
        for cz in range(2):
            rows = []
            for x in range(2):
                for y in range(2):
                    rows.append(
                        jnp.concatenate(
                            [s6[2 * x + a, 2 * y + b, pl.ds(cz, 24, stride=2), :] for a in range(2)],
                            axis=1,
                        )
                    )
            total = total + dot(jnp.concatenate(rows, axis=0).astype(BF16), wm[2 * b + cz])
    n5[:, 48:64, :] = jnp.zeros((2, 16, 128), F32)
    for x in range(2):
        n5[x, 0:48, :] = total[48 * x : 48 * x + 48]
        w5[1, 1, :, 128 * x : 128 * x + 128] = total[48 * x : 48 * x + 48].astype(BF16)

    total = jnp.zeros((16, 128), F32)
    for b in range(2):
        for cz in range(2):
            rows = jnp.concatenate(
                [n5[a, pl.ds(24 * b + cz, 16, stride=2), :] for a in range(2)], axis=1
            )
            total = total + dot(rows.astype(BF16), wm[2 * b + cz])
    depth = lax.broadcasted_iota(jnp.int32, (16, 128), 0)
    w4[1, 1, r % 2, c % 2] = jnp.where(depth < 12, total, 0.0).astype(BF16)

    @pl.when(r == 0)
    def _():
        w6[0] = jnp.zeros_like(w6[0])
        w5[0] = jnp.zeros_like(w5[0])

    @pl.when(r == nr - 1)
    def _():
        w6[3] = jnp.zeros_like(w6[3])
        w5[2] = jnp.zeros_like(w5[2])

    @pl.when(c == 0)
    def _():
        w6[:, 0:2] = jnp.zeros_like(w6[:, 0:2])
        w5[:, 0] = jnp.zeros_like(w5[:, 0])

    @pl.when(c == nc - 1)
    def _():
        w6[:, 6:8] = jnp.zeros_like(w6[:, 6:8])
        w5[:, 2] = jnp.zeros_like(w5[:, 2])

    @pl.when(r // 2 == 0)
    def _():
        w4[0] = jnp.zeros_like(w4[0])

    @pl.when(r // 2 == nr // 2 - 1)
    def _():
        w4[2] = jnp.zeros_like(w4[2])

    @pl.when(c // 2 == 0)
    def _():
        w4[:, 0] = jnp.zeros_like(w4[:, 0])

    @pl.when(c // 2 == nc // 2 - 1)
    def _():
        w4[:, 2] = jnp.zeros_like(w4[:, 2])

    pl.semaphore_wait(barrier, greeted)

    def remote(src, dst, send, recv, rr, cc):
        return pltpu.make_async_remote_copy(
            src_ref=src,
            dst_ref=dst,
            send_sem=send,
            recv_sem=recv,
            device_id={"row": rr, "col": cc},
            device_id_type=MESH,
        )

    def mate_copy(n):
        dr, dc = MATES[n]
        tile = w4.at[1, 1, r % 2, c % 2]
        return remote(
            tile, tile, a_send.at[n], a_recv.at[n], r + dr * (1 - 2 * (r % 2)), c + dc * (1 - 2 * (c % 2))
        )

    def mate_landing(n):
        dr, dc = MATES[n]
        tile = w4.at[1, 1, (r + dr) % 2, (c + dc) % 2]
        return remote(tile, tile, a_send.at[n], a_recv.at[n], r, c)

    def span(d, own, low, high, width):
        if d == 0:
            return pl.ds(own, 2 * width), pl.ds(own, 2 * width)
        if d < 0:
            return pl.ds(own, width), pl.ds(high, width)
        return pl.ds(own + width, width), pl.ds(low, width)

    def rim_copy(n):
        dr, dc = AROUND[n]
        sx, tx = span(dr, 1, 0, 3, 1)
        sy, ty = span(dc, 2, 0, 6, 2)
        return remote(
            w6.at[sx, sy], w6.at[tx, ty], s6_send.at[n], s6_recv.at[n], r + dr, c + dc
        )

    def five_copy(n):
        dr, dc = AROUND[n]
        return remote(
            w5.at[1, 1], w5.at[1 - dr, 1 - dc], s5_send.at[n], s5_recv.at[n], r + dr, c + dc
        )

    def four_copy(n):
        dr, dc = AROUND[n]
        return remote(
            w4.at[1, 1], w4.at[1 - dr, 1 - dc], b_send.at[n], b_recv.at[n], r + 2 * dr, c + 2 * dc
        )

    def sends_to(n, scale):
        dr, dc = AROUND[n]
        return inside(r + scale * dr, c + scale * dc)

    def gets_from(n, scale):
        dr, dc = AROUND[n]
        return inside(r - scale * dr, c - scale * dc)

    def each(make, scale, wanted, act):
        for n in range(8):

            @pl.when(wanted(n, scale))
            def _():
                act(make(n))

    for n in range(3):
        mate_copy(n).start()
    each(five_copy, 1, sends_to, lambda copy: copy.start())
    each(rim_copy, 1, sends_to, lambda copy: copy.start())

    def turn(dx):
        ops_copies[dx].wait()

        for dy in range(7):
            for dz in range(7):
                if all(2 <= d <= 4 for d in (dx, dy, dz)):
                    opt[dx, dy, dz] = jnp.zeros((128, 128), BF16)
                else:
                    opt[dx, dy, dz, 112:128] = jnp.zeros((16, 128), BF16)
                    opt[dx, dy, dz, 0:C, 0:C] = jnp.transpose(ops[dx, dy, dz])

    lf[0 : 8 * C, 0:C] = l2l[...].astype(F32)
    wl[...] = jnp.zeros_like(wl)
    for a in range(2):
        for b in range(2):
            for cz in range(2):
                wl[2 * a + b, 0:C, 128 * cz : 128 * cz + C] = octant(lf, a, b, cz)
    for dx in (0, 1):
        turn(dx)

    for n in range(3):
        mate_landing(n).wait_recv()
    for b in range(2):
        for a in range(2):
            n4[b, a] = w4[1, 1, a, b].astype(F32)
    total = jnp.zeros((16, 128), F32)
    for b in range(2):
        for cz in range(2):
            rows = jnp.concatenate(
                [
                    jnp.concatenate([n4[b, a, pl.ds(cz, 8, stride=2), :] for a in range(2)], axis=1),
                    jnp.zeros((8, 256), F32),
                ],
                axis=0,
            )
            total = total + dot(rows.astype(BF16), wm[2 * b + cz])
    t3[...] = jnp.where(depth < 6, total, 0.0).astype(BF16)

    def three_copy(n):
        rr, cc = partner(n)
        return remote(
            t3,
            m3.at[(r // 2) % 2, (c // 2) % 2, r // 4, c // 4],
            c_send.at[n],
            c_recv.at[4 * (r // 4) + c // 4],
            rr,
            cc,
        )

    def three_landing(n):
        return remote(t3, m3.at[r % 2, c % 2, n // 4, n % 4], c_send.at[n], c_recv.at[n], r, c)

    def is_other(n):
        rr, cc = partner(n)
        return (rr != r) | (cc != c)

    def over_partners(act):
        def step(n, _):
            @pl.when(is_other(n))
            def _():
                act(n)

            return 0

        lax.fori_loop(0, 16, step, 0)

    over_partners(lambda n: three_copy(n).start())

    @pl.when((swap(r % 4) == r % 4) & (swap(c % 4) == c % 4))
    def _():
        m3[r % 2, c % 2, r // 4, c // 4] = t3[...]

    each(four_copy, 2, sends_to, lambda copy: copy.start())

    for dx in (2, 3, 4):
        turn(dx)

    over_partners(lambda n: three_landing(n).wait_recv())

    def share_copy(n):
        dr, dc = MATES[n]
        part = m3.at[r % 2, c % 2]
        return remote(
            part, part, d_send.at[n], d_recv.at[n], r + dr * (1 - 2 * (r % 2)), c + dc * (1 - 2 * (c % 2))
        )

    def share_landing(n):
        dr, dc = MATES[n]
        part = m3.at[(r + dr) % 2, (c + dc) % 2]
        return remote(part, part, d_send.at[n], d_recv.at[n], r, c)

    for n in range(3):
        share_copy(n).start()
    for dx in (5, 6):
        turn(dx)
    for n in range(3):
        share_landing(n).wait_recv()

    for b in range(2):
        for i in range(4):
            for a in range(2):
                n3[b, a, 64 * i : 64 * i + 64] = jnp.concatenate(
                    [m3[a, b, i, j].astype(F32) for j in range(4)], axis=0
                )
    total = jnp.zeros((128, 128), F32)
    for b in range(2):
        for cz in range(2):
            rows = jnp.concatenate(
                [n3[b, a, pl.ds(cz, 128, stride=2), :] for a in range(2)], axis=1
            )
            total = total + dot(rows.astype(BF16), wm[2 * b + cz])
    for n in range(16):
        n2[n // 4, n % 4] = total[8 * n : 8 * n + 8]

    each(four_copy, 2, gets_from, lambda copy: copy.wait_recv())
    each(five_copy, 1, gets_from, lambda copy: copy.wait_recv())
    row8 = lax.broadcasted_iota(jnp.int32, (8, 256), 0)
    from_below = (row8 == 1) | (row8 == 2) | (row8 == 3) | (row8 == 5)
    from_above = (row8 == 0) | (row8 == 1) | (row8 == 2) | (row8 == 4)

    def wide(ref, k):
        return jnp.concatenate([ref[a, pl.ds(k, 8, stride=6), :] for a in range(2)], axis=1)

    def levels(column, below, above):
        v = [column(k) for k in range(6)]
        low = [jnp.where(below, pltpu.roll(v[k], 1, axis=0), 0.0) for k in (4, 5)]
        high = [jnp.where(above, pltpu.roll(v[k], 7, axis=0), 0.0) for k in (0, 1)]
        return low + v + high

    def coarse(n, _):
        x, y = n // 6, n % 6
        half, odd = y // 2, y % 2
        five = w5[x, half].astype(F32)
        five = jnp.where(odd == 0, five[0:24], five[24:48])
        i3, j3 = r // 4 - 1 + x, c // 4 - 1 + half
        ok3 = (i3 >= 0) & (i3 < 4) & (j3 >= 0) & (j3 < 4)
        j2 = 2 * (c // 8) - 2 + y
        for a in range(2):
            nat[a, 0:24] = five[:, 128 * a : 128 * a + 128]
            nat[a, 24:36] = w4[x, half, a, odd].astype(F32)[0:12]
            three = m3[a, odd, jnp.clip(i3, 0, 3), jnp.clip(j3, 0, 3)].astype(F32)
            nat[a, 36:42] = jnp.where(ok3, three[0:6], 0.0)
            i2 = 2 * (r // 8 - 1 + x) + a
            ok2 = (i2 >= 0) & (i2 < 4) & (j2 >= 0) & (j2 < 4)
            two = n2[jnp.clip(i2, 0, 3), jnp.clip(j2, 0, 3)]
            nat[a, 42:48] = jnp.where(ok2, two[0:6], 0.0)
        v = levels(lambda k: wide(nat, k), from_below, from_above)
        for s in range(6):
            ts[x, y, s] = jnp.concatenate(
                [v[s], v[s + 2], v[s + 4], jnp.zeros((8, 256), F32)], axis=0
            ).astype(BF16)
        return 0

    lax.fori_loop(0, 18, coarse, 0)

    each(rim_copy, 1, gets_from, lambda copy: copy.wait_recv())

    def fine(y, _):
        before = None
        for x in range(4):
            whole = w6[x, y].astype(F32)
            for a in range(2):
                col[x, a] = whole[:, 128 * a : 128 * a + 128]
            v = levels(lambda k: wide(col.at[x], k), row8 >= 1, row8 <= 6)
            if before is not None:
                for k in range(10):
                    t6[x - 1, y, k] = jnp.concatenate([before[k], v[k]], axis=0).astype(BF16)
            before = v
        return 0

    lax.fori_loop(0, 8, fine, 0)

    def far(p, _):
        py, pz = p // 2, p % 2
        near = [-1, 0, 1, -2, 2]
        total = jnp.zeros((128, 256), F32)
        for j in range(3):
            for ey in range(6):
                dy = near[ey] if ey < 5 else 3 - 6 * py
                for ez in range(6):
                    dz = near[ez] if ez < 5 else 3 - 6 * pz
                    if j == 1 and ey < 3 and ez < 3:
                        continue
                    y0, k0 = py + dy + 2, pz + dz + 2
                    x = jnp.concatenate(
                        [t6[j, y0 + 2 * t, k0 + 2 * m] for t in range(2) for m in range(3)]
                        + [ts[j, y0, k0]],
                        axis=0,
                    )
                    w = jnp.concatenate(
                        [
                            jnp.concatenate(
                                [opt[2 * j + a - 2 - px + 3, dy + 3, dz + 3] for px in range(2)],
                                axis=1,
                            )
                            for a in range(2)
                        ],
                        axis=0,
                    )
                    total = total + dot(x, w)
        for px in range(2):
            lanes = slice(128 * px, 128 * px + 128)
            for m in range(3):
                zs = pl.ds(2 * m + pz, 8, stride=6)
                for t in range(2):
                    for g in range(2):
                        at = 48 * t + 16 * m + 8 * g
                        f6[2 * g + px, py + 2 * t, zs, :] = total[at : at + 8, lanes]
                fs[px, py, zs, :] = total[96 + 8 * m : 104 + 8 * m, lanes]
        return 0

    lax.fori_loop(0, 4, far, 0)

    def real(parents):
        lane = lax.broadcasted_iota(jnp.int32, parents.shape, 1)
        return jnp.where(lane < C, parents, 0.0).astype(BF16)

    def refine(parents, a, b):
        return dot(real(parents), wl[2 * a + b])

    ls[...] = jnp.zeros_like(ls)
    two = fs[(r // 4) % 2, (c // 4) % 2, 40:48, :]
    ls[0, 0:8] = two
    two = jnp.concatenate([ls[0, 2:8], jnp.zeros((10, 128), F32)], axis=0)
    both = refine(two, (r // 2) % 2, (c // 2) % 2)
    for cz in range(2):
        ls[1, pl.ds(cz, 8, stride=2), :] = both[0:8, 128 * cz : 128 * cz + 128]
    three = ls[1, 0:6] + fs[(r // 2) % 2, (c // 2) % 2, 36:42, :]
    three = jnp.concatenate([three, jnp.zeros((10, 128), F32)], axis=0)
    both = refine(three, r % 2, c % 2)
    for cz in range(2):
        ls[2, pl.ds(cz, 8, stride=2), :] = both[0:8, 128 * cz : 128 * cz + 128]
    four = ls[2, 0:12] + fs[r % 2, c % 2, 24:36, :]
    four = jnp.concatenate([four, jnp.zeros((4, 128), F32)], axis=0)
    fives = []
    for a in range(2):
        for b in range(2):
            both = refine(four, a, b)
            for cz in range(2):
                ls[3 + 2 * a + b, pl.ds(cz, 16, stride=2), :] = both[:, 128 * cz : 128 * cz + 128]
            fives.append(ls[3 + 2 * a + b, 0:24] + fs[a, b, 0:24, :])
    five = real(jnp.concatenate(fives, axis=0))
    for a in range(2):
        for b in range(2):
            both = dot(five, wl[2 * a + b])
            for x in range(2):
                for y in range(2):
                    at = 24 * (2 * x + y)
                    for cz in range(2):
                        zs = pl.ds(cz, 24, stride=2)
                        s6[2 * x + a, 2 * y + b, zs, :] = (
                            f6[2 * x + a, 2 * y + b, zs, :]
                            + both[at : at + 24, 128 * cz : 128 * cz + 128]
                        )
    out[...] = s6[:, :, :, 0:C]

    for n in range(3):
        mate_copy(n).wait_send()
        share_copy(n).wait_send()
    each(five_copy, 1, sends_to, lambda copy: copy.wait_send())
    each(rim_copy, 1, sends_to, lambda copy: copy.wait_send())
    each(four_copy, 2, sends_to, lambda copy: copy.wait_send())
    over_partners(lambda n: three_copy(n).wait_send())


def local(leaf_multipoles, occupancy, m2m_ops, m2l_ops, l2l_ops):
    leaf = jnp.transpose(leaf_multipoles, (1, 2, 3, 0))
    m2m = jnp.transpose(m2m_ops, (0, 1, 3, 2, 4)).reshape(8 * C, C)
    l2l = jnp.transpose(l2l_ops, (0, 1, 3, 2, 4)).reshape(8 * C, C)
    vmem = pl.BlockSpec(memory_space=pltpu.VMEM)
    dma = pltpu.SemaphoreType.DMA
    result = pl.pallas_call(
        kernel,
        out_shape=jax.ShapeDtypeStruct((4, 4, 48, C), F32),
        in_specs=[vmem] * 4 + [pl.BlockSpec(memory_space=pl.ANY)],
        out_specs=vmem,
        scratch_shapes=[
            pltpu.VMEM((7, 7, 7, C, C), BF16),
            pltpu.VMEM((7, 7, 7, 128, 128), BF16),
            pltpu.VMEM((984, 128), F32),
            pltpu.VMEM((4, 256, 128), BF16),
            pltpu.VMEM((984, 128), F32),
            pltpu.VMEM((4, 128, 256), BF16),
            pltpu.VMEM((4, 4, 48, 128), F32),
            pltpu.VMEM((4, 8, 48, 256), BF16),
            pltpu.VMEM((2, 64, 128), F32),
            pltpu.VMEM((3, 3, 48, 256), BF16),
            pltpu.VMEM((3, 3, 2, 2, 16, 128), BF16),
            pltpu.VMEM((2, 2, 16, 128), F32),
            pltpu.VMEM((16, 128), BF16),
            pltpu.VMEM((2, 2, 4, 4, 16, 128), BF16),
            pltpu.VMEM((2, 2, 256, 128), F32),
            pltpu.VMEM((4, 4, 8, 128), F32),
            pltpu.VMEM((2, 48, 128), F32),
            pltpu.VMEM((4, 2, 48, 128), F32),
            pltpu.VMEM((3, 8, 10, 16, 256), BF16),
            pltpu.VMEM((3, 6, 6, 32, 256), BF16),
            pltpu.VMEM((4, 4, 48, 128), F32),
            pltpu.VMEM((2, 2, 48, 128), F32),
            pltpu.VMEM((7, 32, 128), F32),
            dma((7,)),
            dma((8,)),
            dma((8,)),
            dma((8,)),
            dma((8,)),
            dma((3,)),
            dma((3,)),
            dma((8,)),
            dma((8,)),
            dma((16,)),
            dma((16,)),
            dma((3,)),
            dma((3,)),
        ],
        compiler_params=pltpu.CompilerParams(
            collective_id=0, has_side_effects=True, vmem_limit_bytes=56 * 2**20
        ),
    )(leaf, occupancy, m2m, l2l, m2l_ops)
    return jnp.transpose(result, (3, 0, 1, 2))


def solution(mesh):
    placed = (P(None, "row", "col", None), P("row", "col", None), P(), P(), P())
    return jax.shard_map(
        local, mesh=mesh, in_specs=placed, out_specs=P(None, "row", "col", None), check_vma=False
    )
```

```python
import functools

import jax
import jax.numpy as jnp
from jax import lax
from jax.experimental import pallas as pl
from jax.experimental.pallas import tpu as pltpu
from jax.sharding import PartitionSpec as P

MESH = pl.DeviceIdType.MESH
C = 121
F32 = jnp.float32
BF16 = jnp.bfloat16
AROUND = [(dr, dc) for dr in (-1, 0, 1) for dc in (-1, 0, 1) if (dr, dc) != (0, 0)]
MATES = [(0, 1), (1, 0), (1, 1)]


def dot(x, w):
    return jnp.dot(x, w, preferred_element_type=F32)


def swap(v):
    return 2 * (v % 2) + v // 2


def kernel(
    leaf, occ, m2m, l2l, ops_hbm,
    out,
    ops, opt, mf, wm, lf, wl, s6, w6, n5, w5, w4, n4, t3, m3, n3, n2, nat, col, t6, ts, acc, acs, f6, fs, ls,
    ops_sem, s6_send, s6_recv, s5_send, s5_recv, a_send, a_recv, b_send, b_recv,
    c_send, c_recv, d_send, d_recv,
):
    r, c = lax.axis_index("row"), lax.axis_index("col")
    nr, nc = lax.axis_size("row"), lax.axis_size("col")

    ops_copies = [
        pltpu.make_async_copy(ops_hbm.at[dx], ops.at[dx], ops_sem.at[dx]) for dx in range(7)
    ]
    for copy in ops_copies:
        copy.start()

    def inside(rr, cc):
        return (rr >= 0) & (rr < nr) & (cc >= 0) & (cc < nc)

    def partner(n):
        return 4 * (n // 4) + swap(r % 4), 4 * (n % 4) + swap(c % 4)

    barrier = pltpu.get_barrier_semaphore()
    greeted = jnp.int32(0)
    for scale in (1, 2):
        for dr, dc in AROUND:
            rr, cc = r + scale * dr, c + scale * dc
            there = inside(rr, cc)

            @pl.when(there)
            def _():
                pl.semaphore_signal(
                    barrier, inc=1, device_id={"row": rr, "col": cc}, device_id_type=MESH
                )

            greeted = greeted + there.astype(jnp.int32)
    for n in range(16):
        rr, cc = partner(n)
        other = (rr != r) | (cc != c)

        @pl.when(other)
        def _():
            pl.semaphore_signal(
                barrier, inc=1, device_id={"row": rr, "col": cc}, device_id_type=MESH
            )

        greeted = greeted + other.astype(jnp.int32)

    s6[...] = jnp.zeros_like(s6)
    occ_t = jnp.transpose(
        jnp.concatenate([occ[x].astype(F32) for x in range(4)], axis=0)
    )
    for x in range(4):
        for y in range(4):
            here = 4 * x + y
            s6[x, y, :, 0:C] = leaf[x, y] * occ_t[:, here : here + 1]
    for x in range(2):
        for y in range(4):
            for a in range(2):
                w6[1 + x, 2 + y, :, a * 128 : (a + 1) * 128] = s6[2 * x + a, y].astype(BF16)

    def octant(raw, a, b, cz):
        rows = raw[pl.ds((2 * a + b) * 2 * C + cz, 128, stride=2), :]
        return jnp.transpose(rows)[0:C, 0:C].astype(BF16)

    mf[0 : 8 * C, 0:C] = m2m[...].astype(F32)
    wm[...] = jnp.zeros_like(wm)
    for a in range(2):
        for b in range(2):
            for cz in range(2):
                wm[2 * b + cz, 128 * a : 128 * a + C, 0:C] = octant(mf, a, b, cz)

    total = jnp.zeros((96, 128), F32)
    for b in range(2):
        for cz in range(2):
            rows = []
            for x in range(2):
                for y in range(2):
                    rows.append(
                        jnp.concatenate(
                            [s6[2 * x + a, 2 * y + b, pl.ds(cz, 24, stride=2), :] for a in range(2)],
                            axis=1,
                        )
                    )
            total = total + dot(jnp.concatenate(rows, axis=0).astype(BF16), wm[2 * b + cz])
    n5[:, 48:64, :] = jnp.zeros((2, 16, 128), F32)
    for x in range(2):
        n5[x, 0:48, :] = total[48 * x : 48 * x + 48]
        w5[1, 1, :, 128 * x : 128 * x + 128] = total[48 * x : 48 * x + 48].astype(BF16)

    total = jnp.zeros((16, 128), F32)
    for b in range(2):
        for cz in range(2):
            rows = jnp.concatenate(
                [n5[a, pl.ds(24 * b + cz, 16, stride=2), :] for a in range(2)], axis=1
            )
            total = total + dot(rows.astype(BF16), wm[2 * b + cz])
    depth = lax.broadcasted_iota(jnp.int32, (16, 128), 0)
    w4[1, 1, r % 2, c % 2] = jnp.where(depth < 12, total, 0.0).astype(BF16)

    @pl.when(r == 0)
    def _():
        w6[0] = jnp.zeros_like(w6[0])
        w5[0] = jnp.zeros_like(w5[0])

    @pl.when(r == nr - 1)
    def _():
        w6[3] = jnp.zeros_like(w6[3])
        w5[2] = jnp.zeros_like(w5[2])

    @pl.when(c == 0)
    def _():
        w6[:, 0:2] = jnp.zeros_like(w6[:, 0:2])
        w5[:, 0] = jnp.zeros_like(w5[:, 0])

    @pl.when(c == nc - 1)
    def _():
        w6[:, 6:8] = jnp.zeros_like(w6[:, 6:8])
        w5[:, 2] = jnp.zeros_like(w5[:, 2])

    @pl.when(r // 2 == 0)
    def _():
        w4[0] = jnp.zeros_like(w4[0])

    @pl.when(r // 2 == nr // 2 - 1)
    def _():
        w4[2] = jnp.zeros_like(w4[2])

    @pl.when(c // 2 == 0)
    def _():
        w4[:, 0] = jnp.zeros_like(w4[:, 0])

    @pl.when(c // 2 == nc // 2 - 1)
    def _():
        w4[:, 2] = jnp.zeros_like(w4[:, 2])

    pl.semaphore_wait(barrier, greeted)

    def remote(src, dst, send, recv, rr, cc):
        return pltpu.make_async_remote_copy(
            src_ref=src,
            dst_ref=dst,
            send_sem=send,
            recv_sem=recv,
            device_id={"row": rr, "col": cc},
            device_id_type=MESH,
        )

    def mate_copy(n):
        dr, dc = MATES[n]
        tile = w4.at[1, 1, r % 2, c % 2]
        return remote(
            tile, tile, a_send.at[n], a_recv.at[n], r + dr * (1 - 2 * (r % 2)), c + dc * (1 - 2 * (c % 2))
        )

    def mate_landing(n):
        dr, dc = MATES[n]
        tile = w4.at[1, 1, (r + dr) % 2, (c + dc) % 2]
        return remote(tile, tile, a_send.at[n], a_recv.at[n], r, c)

    def span(d, own, low, high, width):
        if d == 0:
            return pl.ds(own, 2 * width), pl.ds(own, 2 * width)
        if d < 0:
            return pl.ds(own, width), pl.ds(high, width)
        return pl.ds(own + width, width), pl.ds(low, width)

    def rim_copy(n):
        dr, dc = AROUND[n]
        sx, tx = span(dr, 1, 0, 3, 1)
        sy, ty = span(dc, 2, 0, 6, 2)
        return remote(
            w6.at[sx, sy], w6.at[tx, ty], s6_send.at[n], s6_recv.at[n], r + dr, c + dc
        )

    def five_copy(n):
        dr, dc = AROUND[n]
        return remote(
            w5.at[1, 1], w5.at[1 - dr, 1 - dc], s5_send.at[n], s5_recv.at[n], r + dr, c + dc
        )

    def four_copy(n):
        dr, dc = AROUND[n]
        return remote(
            w4.at[1, 1], w4.at[1 - dr, 1 - dc], b_send.at[n], b_recv.at[n], r + 2 * dr, c + 2 * dc
        )

    def sends_to(n, scale):
        dr, dc = AROUND[n]
        return inside(r + scale * dr, c + scale * dc)

    def gets_from(n, scale):
        dr, dc = AROUND[n]
        return inside(r - scale * dr, c - scale * dc)

    def each(make, scale, wanted, act, which=range(8)):
        for n in which:

            @pl.when(wanted(n, scale))
            def _():
                act(make(n))

    for n in range(3):
        mate_copy(n).start()
    SIDES = [n for n in range(8) if AROUND[n][0] == 0]
    ENDS = [n for n in range(8) if AROUND[n][1] == 0]
    CORNERS = [n for n in range(8) if AROUND[n][0] != 0 and AROUND[n][1] != 0]

    def start(copy):
        copy.start()

    def wait_recv(copy):
        copy.wait_recv()

    each(rim_copy, 1, sends_to, start, ENDS)
    each(five_copy, 1, sends_to, start)
    each(rim_copy, 1, sends_to, start, SIDES + CORNERS)

    def turn(dx):
        ops_copies[dx].wait()

        for dy in range(7):
            for dz in range(7):
                if all(2 <= d <= 4 for d in (dx, dy, dz)):
                    opt[dx, dy, dz] = jnp.zeros((128, 128), BF16)
                else:
                    opt[dx, dy, dz, 112:128] = jnp.zeros((16, 128), BF16)
                    opt[dx, dy, dz, 0:C, 0:C] = jnp.transpose(ops[dx, dy, dz])

    lf[0 : 8 * C, 0:C] = l2l[...].astype(F32)
    wl[...] = jnp.zeros_like(wl)
    for a in range(2):
        for b in range(2):
            for cz in range(2):
                wl[2 * a + b, 0:C, 128 * cz : 128 * cz + C] = octant(lf, a, b, cz)
    acc[...] = jnp.zeros_like(acc)
    acs[...] = jnp.zeros_like(acs)
    ls[...] = jnp.zeros_like(ls)
    for dx in (0, 1):
        turn(dx)

    for n in range(3):
        mate_landing(n).wait_recv()
    for b in range(2):
        for a in range(2):
            n4[b, a] = w4[1, 1, a, b].astype(F32)
    total = jnp.zeros((16, 128), F32)
    for b in range(2):
        for cz in range(2):
            rows = jnp.concatenate(
                [
                    jnp.concatenate([n4[b, a, pl.ds(cz, 8, stride=2), :] for a in range(2)], axis=1),
                    jnp.zeros((8, 256), F32),
                ],
                axis=0,
            )
            total = total + dot(rows.astype(BF16), wm[2 * b + cz])
    t3[...] = jnp.where(depth < 6, total, 0.0).astype(BF16)

    def three_copy(n):
        rr, cc = partner(n)
        return remote(
            t3,
            m3.at[(r // 2) % 2, (c // 2) % 2, r // 4, c // 4],
            c_send.at[n],
            c_recv.at[4 * (r // 4) + c // 4],
            rr,
            cc,
        )

    def three_landing(n):
        return remote(t3, m3.at[r % 2, c % 2, n // 4, n % 4], c_send.at[n], c_recv.at[n], r, c)

    def is_other(n):
        rr, cc = partner(n)
        return (rr != r) | (cc != c)

    def over_partners(act):
        def step(n, _):
            @pl.when(is_other(n))
            def _():
                act(n)

            return 0

        lax.fori_loop(0, 16, step, 0)

    over_partners(lambda n: three_copy(n).start())

    @pl.when((swap(r % 4) == r % 4) & (swap(c % 4) == c % 4))
    def _():
        m3[r % 2, c % 2, r // 4, c // 4] = t3[...]

    each(four_copy, 2, sends_to, lambda copy: copy.start())

    for dx in (2, 3, 4, 5, 6):
        turn(dx)

    over_partners(lambda n: three_landing(n).wait_recv())

    def share_copy(n):
        dr, dc = MATES[n]
        part = m3.at[r % 2, c % 2]
        return remote(
            part, part, d_send.at[n], d_recv.at[n], r + dr * (1 - 2 * (r % 2)), c + dc * (1 - 2 * (c % 2))
        )

    def share_landing(n):
        dr, dc = MATES[n]
        part = m3.at[(r + dr) % 2, (c + dc) % 2]
        return remote(part, part, d_send.at[n], d_recv.at[n], r, c)

    for n in range(3):
        share_copy(n).start()
    row8 = lax.broadcasted_iota(jnp.int32, (8, 256), 0)
    from_below = (row8 == 1) | (row8 == 2) | (row8 == 3) | (row8 == 5)
    from_above = (row8 == 0) | (row8 == 1) | (row8 == 2) | (row8 == 4)

    def wide(ref, k):
        return jnp.concatenate([ref[a, pl.ds(k, 8, stride=6), :] for a in range(2)], axis=1)

    def levels(column, below, above):
        v = [column(k) for k in range(6)]
        low = [jnp.where(below, pltpu.roll(v[k], 1, axis=0), 0.0) for k in (4, 5)]
        high = [jnp.where(above, pltpu.roll(v[k], 7, axis=0), 0.0) for k in (0, 1)]
        return low + v + high

    def fine(x, y):
        whole = w6[x, y].astype(F32)
        for a in range(2):
            col[x, a] = whole[:, 128 * a : 128 * a + 128]
        return levels(lambda k: wide(col.at[x], k), row8 >= 1, row8 <= 6)

    def pair(x, y):
        low, high = fine(x, y), fine(x + 1, y)
        for k in range(10):
            t6[x, y, k] = jnp.concatenate([low[k], high[k]], axis=0).astype(BF16)

    def pairs(xs, ys):
        def step(n, _):
            for x in xs:
                pair(x, ys(n))
            return 0

        return step

    def far(own, small):
        for dy in range(-3, 4):
            for dz in range(-3, 4):
                use = [j for j in range(3) if j != 1 or max(abs(dy), abs(dz)) > 1]
                tys = range(4) if abs(dy) < 3 else (0, 2) if dy > 0 else (1, 3)
                tys = [ty for ty in tys if (0 <= ty + dy <= 3) == own]
                if not tys and not small:
                    continue
                tks = range(6) if abs(dz) < 3 else (0, 2, 4) if dz > 0 else (1, 3, 5)
                w = jnp.concatenate(
                    [
                        jnp.concatenate(
                            [opt[2 * j + a - px + 1, dy + 3, dz + 3] for px in range(2)], axis=1
                        )
                        for j in use
                        for a in range(2)
                    ],
                    axis=0,
                )
                rows, sums = [], []
                for ty in tys:
                    for k in tks:
                        rows.append([t6[j, ty + dy + 2, k + dz + 2] for j in use])
                        sums.append(acc.at[ty, k])
                if small:
                    for k in tks:
                        rows.append([ts[j, dy + 3, k + dz + 2] for j in use])
                        sums.append(acs.at[k])
                total = dot(
                    jnp.concatenate([jnp.concatenate(row, axis=1) for row in rows], axis=0), w
                )
                for n, tile in enumerate(sums):
                    tile[...] += total[16 * n : 16 * n + 16]


    each(rim_copy, 1, gets_from, wait_recv, ENDS)
    lax.fori_loop(2, 6, pairs([0, 1, 2], lambda n: n), 0)
    far(True, False)
    for n in range(3):
        share_landing(n).wait_recv()

    for b in range(2):
        for i in range(4):
            for a in range(2):
                n3[b, a, 64 * i : 64 * i + 64] = jnp.concatenate(
                    [m3[a, b, i, j].astype(F32) for j in range(4)], axis=0
                )
    total = jnp.zeros((128, 128), F32)
    for b in range(2):
        for cz in range(2):
            rows = jnp.concatenate(
                [n3[b, a, pl.ds(cz, 128, stride=2), :] for a in range(2)], axis=1
            )
            total = total + dot(rows.astype(BF16), wm[2 * b + cz])
    for n in range(16):
        n2[n // 4, n % 4] = total[8 * n : 8 * n + 8]

    each(four_copy, 2, gets_from, lambda copy: copy.wait_recv())
    each(five_copy, 1, gets_from, lambda copy: copy.wait_recv())
    def coarse(x, y):
        half, odd = y // 2, y % 2
        five = w5[x, half].astype(F32)
        five = five[24 * odd : 24 * odd + 24]
        i3, j3 = r // 4 - 1 + x, c // 4 - 1 + half
        ok3 = (i3 >= 0) & (i3 < 4) & (j3 >= 0) & (j3 < 4)
        j2 = 2 * (c // 8) - 2 + y
        for a in range(2):
            nat[a, 0:24] = five[:, 128 * a : 128 * a + 128]
            nat[a, 24:36] = w4[x, half, a, odd].astype(F32)[0:12]
            three = m3[a, odd, jnp.clip(i3, 0, 3), jnp.clip(j3, 0, 3)].astype(F32)
            nat[a, 36:42] = jnp.where(ok3, three[0:6], 0.0)
            i2 = 2 * (r // 8 - 1 + x) + a
            ok2 = (i2 >= 0) & (i2 < 4) & (j2 >= 0) & (j2 < 4)
            two = n2[jnp.clip(i2, 0, 3), jnp.clip(j2, 0, 3)]
            nat[a, 42:48] = jnp.where(ok2, two[0:6], 0.0)
        return levels(lambda k: wide(nat, k), from_below, from_above)

    def small_windows(x, _):
        nothing = [jnp.zeros((8, 256), F32)] * 10
        before = nothing
        for y in range(7):
            now = coarse(x, y) if y < 6 else nothing
            for k in range(10):
                ts[x, y, k] = jnp.concatenate([before[k], now[k]], axis=0).astype(BF16)
            before = now
        return 0

    lax.fori_loop(0, 3, small_windows, 0)

    each(rim_copy, 1, gets_from, wait_recv, SIDES + CORNERS)
    lax.fori_loop(0, 4, pairs([0, 1, 2], lambda n: n + 4 * (n // 2)), 0)
    far(False, True)
    for k in range(6):
        zs = pl.ds(k, 8, stride=6)
        for px in range(2):
            lanes = slice(128 * px, 128 * px + 128)
            for g in range(2):
                for ty in range(4):
                    f6[2 * g + px, ty, zs, :] = acc[ty, k, 8 * g : 8 * g + 8, lanes]
            for py in range(2):
                fs[px, py, zs, :] = acs[k, 8 * py : 8 * py + 8, lanes]

    def real(parents):
        lane = lax.broadcasted_iota(jnp.int32, parents.shape, 1)
        return jnp.where(lane < C, parents, 0.0).astype(BF16)

    def refine(parents, a, b):
        return dot(real(parents), wl[2 * a + b])

    two = fs[(r // 4) % 2, (c // 4) % 2, 40:48, :]
    ls[0, 0:8] = two
    two = jnp.concatenate([ls[0, 2:8], jnp.zeros((10, 128), F32)], axis=0)
    both = refine(two, (r // 2) % 2, (c // 2) % 2)
    for cz in range(2):
        ls[1, pl.ds(cz, 8, stride=2), :] = both[0:8, 128 * cz : 128 * cz + 128]
    three = ls[1, 0:6] + fs[(r // 2) % 2, (c // 2) % 2, 36:42, :]
    three = jnp.concatenate([three, jnp.zeros((10, 128), F32)], axis=0)
    both = refine(three, r % 2, c % 2)
    for cz in range(2):
        ls[2, pl.ds(cz, 8, stride=2), :] = both[0:8, 128 * cz : 128 * cz + 128]
    four = ls[2, 0:12] + fs[r % 2, c % 2, 24:36, :]
    four = jnp.concatenate([four, jnp.zeros((4, 128), F32)], axis=0)
    fives = []
    for a in range(2):
        for b in range(2):
            both = refine(four, a, b)
            for cz in range(2):
                ls[3 + 2 * a + b, pl.ds(cz, 16, stride=2), :] = both[:, 128 * cz : 128 * cz + 128]
            fives.append(ls[3 + 2 * a + b, 0:24] + fs[a, b, 0:24, :])
    five = real(jnp.concatenate(fives, axis=0))
    for a in range(2):
        for b in range(2):
            both = dot(five, wl[2 * a + b])
            for x in range(2):
                for y in range(2):
                    at = 24 * (2 * x + y)
                    for cz in range(2):
                        zs = pl.ds(cz, 24, stride=2)
                        s6[2 * x + a, 2 * y + b, zs, :] = (
                            f6[2 * x + a, 2 * y + b, zs, :]
                            + both[at : at + 24, 128 * cz : 128 * cz + 128]
                        )
    out[...] = s6[:, :, :, 0:C]

    for n in range(3):
        mate_copy(n).wait_send()
        share_copy(n).wait_send()
    each(five_copy, 1, sends_to, lambda copy: copy.wait_send())
    each(rim_copy, 1, sends_to, lambda copy: copy.wait_send())
    each(four_copy, 2, sends_to, lambda copy: copy.wait_send())
    over_partners(lambda n: three_copy(n).wait_send())


def local(leaf_multipoles, occupancy, m2m_ops, m2l_ops, l2l_ops):
    leaf = jnp.transpose(leaf_multipoles, (1, 2, 3, 0))
    m2m = jnp.transpose(m2m_ops, (0, 1, 3, 2, 4)).reshape(8 * C, C)
    l2l = jnp.transpose(l2l_ops, (0, 1, 3, 2, 4)).reshape(8 * C, C)
    vmem = pl.BlockSpec(memory_space=pltpu.VMEM)
    dma = pltpu.SemaphoreType.DMA
    result = pl.pallas_call(
        kernel,
        out_shape=jax.ShapeDtypeStruct((4, 4, 48, C), F32),
        in_specs=[vmem] * 4 + [pl.BlockSpec(memory_space=pl.ANY)],
        out_specs=vmem,
        scratch_shapes=[
            pltpu.VMEM((7, 7, 7, C, C), BF16),
            pltpu.VMEM((7, 7, 7, 128, 128), BF16),
            pltpu.VMEM((984, 128), F32),
            pltpu.VMEM((4, 256, 128), BF16),
            pltpu.VMEM((984, 128), F32),
            pltpu.VMEM((4, 128, 256), BF16),
            pltpu.VMEM((4, 4, 48, 128), F32),
            pltpu.VMEM((4, 8, 48, 256), BF16),
            pltpu.VMEM((2, 64, 128), F32),
            pltpu.VMEM((3, 3, 48, 256), BF16),
            pltpu.VMEM((3, 3, 2, 2, 16, 128), BF16),
            pltpu.VMEM((2, 2, 16, 128), F32),
            pltpu.VMEM((16, 128), BF16),
            pltpu.VMEM((2, 2, 4, 4, 16, 128), BF16),
            pltpu.VMEM((2, 2, 256, 128), F32),
            pltpu.VMEM((4, 4, 8, 128), F32),
            pltpu.VMEM((2, 48, 128), F32),
            pltpu.VMEM((4, 2, 48, 128), F32),
            pltpu.VMEM((3, 8, 10, 16, 256), BF16),
            pltpu.VMEM((3, 7, 10, 16, 256), BF16),
            pltpu.VMEM((4, 6, 16, 256), F32),
            pltpu.VMEM((6, 16, 256), F32),
            pltpu.VMEM((4, 4, 48, 128), F32),
            pltpu.VMEM((2, 2, 48, 128), F32),
            pltpu.VMEM((7, 32, 128), F32),
            dma((7,)),
            dma((8,)),
            dma((8,)),
            dma((8,)),
            dma((8,)),
            dma((3,)),
            dma((3,)),
            dma((8,)),
            dma((8,)),
            dma((16,)),
            dma((16,)),
            dma((3,)),
            dma((3,)),
        ],
        compiler_params=pltpu.CompilerParams(
            collective_id=0, has_side_effects=True, vmem_limit_bytes=56 * 2**20
        ),
    )(leaf, occupancy, m2m, l2l, m2l_ops)
    return jnp.transpose(result, (3, 0, 1, 2))


def solution(mesh):
    placed = (P(None, "row", "col", None), P("row", "col", None), P(), P(), P())
    return jax.shard_map(
        local, mesh=mesh, in_specs=placed, out_specs=P(None, "row", "col", None), check_vma=False
    )
```

```python
import functools

import jax
import jax.numpy as jnp
from jax import lax
from jax.experimental import pallas as pl
from jax.experimental.pallas import tpu as pltpu
from jax.sharding import PartitionSpec as P

MESH = pl.DeviceIdType.MESH
C = 121
F32 = jnp.float32
BF16 = jnp.bfloat16
AROUND = [(dr, dc) for dr in (-1, 0, 1) for dc in (-1, 0, 1) if (dr, dc) != (0, 0)]
MATES = [(0, 1), (1, 0), (1, 1)]


def dot(x, w):
    return jnp.dot(x, w, preferred_element_type=F32)


def swap(v):
    return 2 * (v % 2) + v // 2


def kernel(
    leaf, occ, m2m, l2l, ops_hbm,
    out,
    ops, opt, mf, wm, lf, wl, s6, w6, n5, w5, w4, n4, t3, m3, n3, n2, nat, col, t6, ts, acc, acs, f6, fs, ls,
    ops_sem, s6_send, s6_recv, s5_send, s5_recv, a_send, a_recv, b_send, b_recv,
    c_send, c_recv, d_send, d_recv,
):
    r, c = lax.axis_index("row"), lax.axis_index("col")
    nr, nc = lax.axis_size("row"), lax.axis_size("col")

    ops_copies = [
        pltpu.make_async_copy(ops_hbm.at[dx], ops.at[dx], ops_sem.at[dx]) for dx in range(7)
    ]
    for copy in ops_copies:
        copy.start()

    def inside(rr, cc):
        return (rr >= 0) & (rr < nr) & (cc >= 0) & (cc < nc)

    def partner(n):
        return 4 * (n // 4) + swap(r % 4), 4 * (n % 4) + swap(c % 4)

    barrier = pltpu.get_barrier_semaphore()
    greeted = jnp.int32(0)
    for scale in (1, 2):
        for dr, dc in AROUND:
            rr, cc = r + scale * dr, c + scale * dc
            there = inside(rr, cc)

            @pl.when(there)
            def _():
                pl.semaphore_signal(
                    barrier, inc=1, device_id={"row": rr, "col": cc}, device_id_type=MESH
                )

            greeted = greeted + there.astype(jnp.int32)
    for n in range(16):
        rr, cc = partner(n)
        other = (rr != r) | (cc != c)

        @pl.when(other)
        def _():
            pl.semaphore_signal(
                barrier, inc=1, device_id={"row": rr, "col": cc}, device_id_type=MESH
            )

        greeted = greeted + other.astype(jnp.int32)

    s6[...] = jnp.zeros_like(s6)
    occ_t = jnp.transpose(
        jnp.concatenate([occ[x].astype(F32) for x in range(4)], axis=0)
    )
    for x in range(4):
        for y in range(4):
            here = 4 * x + y
            s6[x, y, :, 0:C] = leaf[x, y] * occ_t[:, here : here + 1]
    for x in range(2):
        for y in range(4):
            for a in range(2):
                w6[1 + x, 2 + y, :, a * 128 : (a + 1) * 128] = s6[2 * x + a, y].astype(BF16)

    def octant(raw, a, b, cz):
        rows = raw[pl.ds((2 * a + b) * 2 * C + cz, 128, stride=2), :]
        return jnp.transpose(rows)[0:C, 0:C].astype(BF16)

    mf[0 : 8 * C, 0:C] = m2m[...].astype(F32)
    wm[...] = jnp.zeros_like(wm)
    for a in range(2):
        for b in range(2):
            for cz in range(2):
                wm[2 * b + cz, 128 * a : 128 * a + C, 0:C] = octant(mf, a, b, cz)

    total = jnp.zeros((96, 128), F32)
    for b in range(2):
        for cz in range(2):
            rows = []
            for x in range(2):
                for y in range(2):
                    rows.append(
                        jnp.concatenate(
                            [s6[2 * x + a, 2 * y + b, pl.ds(cz, 24, stride=2), :] for a in range(2)],
                            axis=1,
                        )
                    )
            total = total + dot(jnp.concatenate(rows, axis=0).astype(BF16), wm[2 * b + cz])
    n5[:, 48:64, :] = jnp.zeros((2, 16, 128), F32)
    for x in range(2):
        n5[x, 0:48, :] = total[48 * x : 48 * x + 48]
        w5[1, 1, :, 128 * x : 128 * x + 128] = total[48 * x : 48 * x + 48].astype(BF16)

    total = jnp.zeros((16, 128), F32)
    for b in range(2):
        for cz in range(2):
            rows = jnp.concatenate(
                [n5[a, pl.ds(24 * b + cz, 16, stride=2), :] for a in range(2)], axis=1
            )
            total = total + dot(rows.astype(BF16), wm[2 * b + cz])
    depth = lax.broadcasted_iota(jnp.int32, (16, 128), 0)
    w4[1, 1, r % 2, c % 2] = jnp.where(depth < 12, total, 0.0).astype(BF16)

    @pl.when(r == 0)
    def _():
        w6[0] = jnp.zeros_like(w6[0])
        w5[0] = jnp.zeros_like(w5[0])

    @pl.when(r == nr - 1)
    def _():
        w6[3] = jnp.zeros_like(w6[3])
        w5[2] = jnp.zeros_like(w5[2])

    @pl.when(c == 0)
    def _():
        w6[:, 0:2] = jnp.zeros_like(w6[:, 0:2])
        w5[:, 0] = jnp.zeros_like(w5[:, 0])

    @pl.when(c == nc - 1)
    def _():
        w6[:, 6:8] = jnp.zeros_like(w6[:, 6:8])
        w5[:, 2] = jnp.zeros_like(w5[:, 2])

    @pl.when(r // 2 == 0)
    def _():
        w4[0] = jnp.zeros_like(w4[0])

    @pl.when(r // 2 == nr // 2 - 1)
    def _():
        w4[2] = jnp.zeros_like(w4[2])

    @pl.when(c // 2 == 0)
    def _():
        w4[:, 0] = jnp.zeros_like(w4[:, 0])

    @pl.when(c // 2 == nc // 2 - 1)
    def _():
        w4[:, 2] = jnp.zeros_like(w4[:, 2])

    pl.semaphore_wait(barrier, greeted)

    def remote(src, dst, send, recv, rr, cc):
        return pltpu.make_async_remote_copy(
            src_ref=src,
            dst_ref=dst,
            send_sem=send,
            recv_sem=recv,
            device_id={"row": rr, "col": cc},
            device_id_type=MESH,
        )

    def mate_copy(n):
        dr, dc = MATES[n]
        tile = w4.at[1, 1, r % 2, c % 2]
        return remote(
            tile, tile, a_send.at[n], a_recv.at[n], r + dr * (1 - 2 * (r % 2)), c + dc * (1 - 2 * (c % 2))
        )

    def mate_landing(n):
        dr, dc = MATES[n]
        tile = w4.at[1, 1, (r + dr) % 2, (c + dc) % 2]
        return remote(tile, tile, a_send.at[n], a_recv.at[n], r, c)

    def span(d, own, low, high, width):
        if d == 0:
            return pl.ds(own, 2 * width), pl.ds(own, 2 * width)
        if d < 0:
            return pl.ds(own, width), pl.ds(high, width)
        return pl.ds(own + width, width), pl.ds(low, width)

    def rim_copy(n):
        dr, dc = AROUND[n]
        sx, tx = span(dr, 1, 0, 3, 1)
        sy, ty = span(dc, 2, 0, 6, 2)
        return remote(
            w6.at[sx, sy], w6.at[tx, ty], s6_send.at[n], s6_recv.at[n], r + dr, c + dc
        )

    def five_copy(n):
        dr, dc = AROUND[n]
        return remote(
            w5.at[1, 1], w5.at[1 - dr, 1 - dc], s5_send.at[n], s5_recv.at[n], r + dr, c + dc
        )

    def four_copy(n):
        dr, dc = AROUND[n]
        return remote(
            w4.at[1, 1], w4.at[1 - dr, 1 - dc], b_send.at[n], b_recv.at[n], r + 2 * dr, c + 2 * dc
        )

    def sends_to(n, scale):
        dr, dc = AROUND[n]
        return inside(r + scale * dr, c + scale * dc)

    def gets_from(n, scale):
        dr, dc = AROUND[n]
        return inside(r - scale * dr, c - scale * dc)

    def each(make, scale, wanted, act, which=range(8)):
        for n in which:

            @pl.when(wanted(n, scale))
            def _():
                act(make(n))

    for n in range(3):
        mate_copy(n).start()
    SIDES = [n for n in range(8) if AROUND[n][0] == 0]
    ENDS = [n for n in range(8) if AROUND[n][1] == 0]
    CORNERS = [n for n in range(8) if AROUND[n][0] != 0 and AROUND[n][1] != 0]

    def start(copy):
        copy.start()

    def wait_recv(copy):
        copy.wait_recv()

    each(rim_copy, 1, sends_to, start, SIDES + ENDS)

    def turn(dx):
        ops_copies[dx].wait()

        for dy in range(7):
            for dz in range(7):
                if all(2 <= d <= 4 for d in (dx, dy, dz)):
                    opt[dx, dy, dz] = jnp.zeros((128, 128), BF16)
                else:
                    opt[dx, dy, dz, 112:128] = jnp.zeros((16, 128), BF16)
                    opt[dx, dy, dz, 0:C, 0:C] = jnp.transpose(ops[dx, dy, dz])

    lf[0 : 8 * C, 0:C] = l2l[...].astype(F32)
    wl[...] = jnp.zeros_like(wl)
    for a in range(2):
        for b in range(2):
            for cz in range(2):
                wl[2 * a + b, 0:C, 128 * cz : 128 * cz + C] = octant(lf, a, b, cz)
    acc[...] = jnp.zeros_like(acc)
    acs[...] = jnp.zeros_like(acs)
    ls[...] = jnp.zeros_like(ls)
    for dx in (0, 1):
        turn(dx)

    for n in range(3):
        mate_landing(n).wait_recv()
    for b in range(2):
        for a in range(2):
            n4[b, a] = w4[1, 1, a, b].astype(F32)
    total = jnp.zeros((16, 128), F32)
    for b in range(2):
        for cz in range(2):
            rows = jnp.concatenate(
                [
                    jnp.concatenate([n4[b, a, pl.ds(cz, 8, stride=2), :] for a in range(2)], axis=1),
                    jnp.zeros((8, 256), F32),
                ],
                axis=0,
            )
            total = total + dot(rows.astype(BF16), wm[2 * b + cz])
    t3[...] = jnp.where(depth < 6, total, 0.0).astype(BF16)

    def three_copy(n):
        rr, cc = partner(n)
        return remote(
            t3,
            m3.at[(r // 2) % 2, (c // 2) % 2, r // 4, c // 4],
            c_send.at[n],
            c_recv.at[4 * (r // 4) + c // 4],
            rr,
            cc,
        )

    def three_landing(n):
        return remote(t3, m3.at[r % 2, c % 2, n // 4, n % 4], c_send.at[n], c_recv.at[n], r, c)

    def is_other(n):
        rr, cc = partner(n)
        return (rr != r) | (cc != c)

    def over_partners(act):
        def step(n, _):
            @pl.when(is_other(n))
            def _():
                act(n)

            return 0

        lax.fori_loop(0, 16, step, 0)

    over_partners(lambda n: three_copy(n).start())
    each(rim_copy, 1, sends_to, start, CORNERS)
    each(five_copy, 1, sends_to, start)

    @pl.when((swap(r % 4) == r % 4) & (swap(c % 4) == c % 4))
    def _():
        m3[r % 2, c % 2, r // 4, c // 4] = t3[...]

    each(four_copy, 2, sends_to, lambda copy: copy.start())

    for dx in (2, 3, 4, 5, 6):
        turn(dx)

    over_partners(lambda n: three_landing(n).wait_recv())

    def share_copy(n):
        dr, dc = MATES[n]
        part = m3.at[r % 2, c % 2]
        return remote(
            part, part, d_send.at[n], d_recv.at[n], r + dr * (1 - 2 * (r % 2)), c + dc * (1 - 2 * (c % 2))
        )

    def share_landing(n):
        dr, dc = MATES[n]
        part = m3.at[(r + dr) % 2, (c + dc) % 2]
        return remote(part, part, d_send.at[n], d_recv.at[n], r, c)

    for n in range(3):
        share_copy(n).start()
    row8 = lax.broadcasted_iota(jnp.int32, (8, 256), 0)
    from_below = (row8 == 1) | (row8 == 2) | (row8 == 3) | (row8 == 5)
    from_above = (row8 == 0) | (row8 == 1) | (row8 == 2) | (row8 == 4)

    def wide(ref, k):
        return jnp.concatenate([ref[a, pl.ds(k, 8, stride=6), :] for a in range(2)], axis=1)

    def levels(column, below, above):
        v = [column(k) for k in range(6)]
        low = [jnp.where(below, pltpu.roll(v[k], 1, axis=0), 0.0) for k in (4, 5)]
        high = [jnp.where(above, pltpu.roll(v[k], 7, axis=0), 0.0) for k in (0, 1)]
        return low + v + high

    def fine(x, y):
        whole = w6[x, y].astype(F32)
        for a in range(2):
            col[x, a] = whole[:, 128 * a : 128 * a + 128]
        return levels(lambda k: wide(col.at[x], k), row8 >= 1, row8 <= 6)

    def pair(x, y):
        low, high = fine(x, y), fine(x + 1, y)
        for k in range(10):
            t6[x, y, k] = jnp.concatenate([low[k], high[k]], axis=0).astype(BF16)

    def pairs(xs, ys):
        def step(n, _):
            for x in xs:
                pair(x, ys(n))
            return 0

        return step

    def far(own, small):
        for dy in range(-3, 4):
            for dz in range(-3, 4):
                use = [j for j in range(3) if j != 1 or max(abs(dy), abs(dz)) > 1]
                tys = range(4) if abs(dy) < 3 else (0, 2) if dy > 0 else (1, 3)
                tys = [ty for ty in tys if (0 <= ty + dy <= 3) == own]
                if not tys and not small:
                    continue
                tks = range(6) if abs(dz) < 3 else (0, 2, 4) if dz > 0 else (1, 3, 5)
                w = jnp.concatenate(
                    [
                        jnp.concatenate(
                            [opt[2 * j + a - px + 1, dy + 3, dz + 3] for px in range(2)], axis=1
                        )
                        for j in use
                        for a in range(2)
                    ],
                    axis=0,
                )
                rows, sums = [], []
                for ty in tys:
                    for k in tks:
                        rows.append([t6[j, ty + dy + 2, k + dz + 2] for j in use])
                        sums.append(acc.at[ty, k])
                if small:
                    for k in tks:
                        rows.append([ts[j, dy + 3, k + dz + 2] for j in use])
                        sums.append(acs.at[k])
                total = dot(
                    jnp.concatenate([jnp.concatenate(row, axis=1) for row in rows], axis=0), w
                )
                for n, tile in enumerate(sums):
                    tile[...] += total[16 * n : 16 * n + 16]


    each(rim_copy, 1, gets_from, wait_recv, ENDS)
    lax.fori_loop(2, 6, pairs([0, 1, 2], lambda n: n), 0)
    far(True, False)
    for n in range(3):
        share_landing(n).wait_recv()

    for b in range(2):
        for i in range(4):
            for a in range(2):
                n3[b, a, 64 * i : 64 * i + 64] = jnp.concatenate(
                    [m3[a, b, i, j].astype(F32) for j in range(4)], axis=0
                )
    total = jnp.zeros((128, 128), F32)
    for b in range(2):
        for cz in range(2):
            rows = jnp.concatenate(
                [n3[b, a, pl.ds(cz, 128, stride=2), :] for a in range(2)], axis=1
            )
            total = total + dot(rows.astype(BF16), wm[2 * b + cz])
    for n in range(16):
        n2[n // 4, n % 4] = total[8 * n : 8 * n + 8]

    each(four_copy, 2, gets_from, lambda copy: copy.wait_recv())
    each(five_copy, 1, gets_from, lambda copy: copy.wait_recv())
    def coarse(x, y):
        half, odd = y // 2, y % 2
        five = w5[x, half].astype(F32)
        five = five[24 * odd : 24 * odd + 24]
        i3, j3 = r // 4 - 1 + x, c // 4 - 1 + half
        ok3 = (i3 >= 0) & (i3 < 4) & (j3 >= 0) & (j3 < 4)
        j2 = 2 * (c // 8) - 2 + y
        for a in range(2):
            nat[a, 0:24] = five[:, 128 * a : 128 * a + 128]
            nat[a, 24:36] = w4[x, half, a, odd].astype(F32)[0:12]
            three = m3[a, odd, jnp.clip(i3, 0, 3), jnp.clip(j3, 0, 3)].astype(F32)
            nat[a, 36:42] = jnp.where(ok3, three[0:6], 0.0)
            i2 = 2 * (r // 8 - 1 + x) + a
            ok2 = (i2 >= 0) & (i2 < 4) & (j2 >= 0) & (j2 < 4)
            two = n2[jnp.clip(i2, 0, 3), jnp.clip(j2, 0, 3)]
            nat[a, 42:48] = jnp.where(ok2, two[0:6], 0.0)
        return levels(lambda k: wide(nat, k), from_below, from_above)

    def small_windows(x, _):
        nothing = [jnp.zeros((8, 256), F32)] * 10
        before = nothing
        for y in range(7):
            now = coarse(x, y) if y < 6 else nothing
            for k in range(10):
                ts[x, y, k] = jnp.concatenate([before[k], now[k]], axis=0).astype(BF16)
            before = now
        return 0

    lax.fori_loop(0, 3, small_windows, 0)

    each(rim_copy, 1, gets_from, wait_recv, SIDES + CORNERS)
    lax.fori_loop(0, 4, pairs([0, 1, 2], lambda n: n + 4 * (n // 2)), 0)
    far(False, True)
    for k in range(6):
        zs = pl.ds(k, 8, stride=6)
        for px in range(2):
            lanes = slice(128 * px, 128 * px + 128)
            for g in range(2):
                for ty in range(4):
                    f6[2 * g + px, ty, zs, :] = acc[ty, k, 8 * g : 8 * g + 8, lanes]
            for py in range(2):
                fs[px, py, zs, :] = acs[k, 8 * py : 8 * py + 8, lanes]

    def real(parents):
        lane = lax.broadcasted_iota(jnp.int32, parents.shape, 1)
        return jnp.where(lane < C, parents, 0.0).astype(BF16)

    def refine(parents, a, b):
        return dot(real(parents), wl[2 * a + b])

    two = fs[(r // 4) % 2, (c // 4) % 2, 40:48, :]
    ls[0, 0:8] = two
    two = jnp.concatenate([ls[0, 2:8], jnp.zeros((10, 128), F32)], axis=0)
    both = refine(two, (r // 2) % 2, (c // 2) % 2)
    for cz in range(2):
        ls[1, pl.ds(cz, 8, stride=2), :] = both[0:8, 128 * cz : 128 * cz + 128]
    three = ls[1, 0:6] + fs[(r // 2) % 2, (c // 2) % 2, 36:42, :]
    three = jnp.concatenate([three, jnp.zeros((10, 128), F32)], axis=0)
    both = refine(three, r % 2, c % 2)
    for cz in range(2):
        ls[2, pl.ds(cz, 8, stride=2), :] = both[0:8, 128 * cz : 128 * cz + 128]
    four = ls[2, 0:12] + fs[r % 2, c % 2, 24:36, :]
    four = jnp.concatenate([four, jnp.zeros((4, 128), F32)], axis=0)
    fives = []
    for a in range(2):
        for b in range(2):
            both = refine(four, a, b)
            for cz in range(2):
                ls[3 + 2 * a + b, pl.ds(cz, 16, stride=2), :] = both[:, 128 * cz : 128 * cz + 128]
            fives.append(ls[3 + 2 * a + b, 0:24] + fs[a, b, 0:24, :])
    five = real(jnp.concatenate(fives, axis=0))
    for a in range(2):
        for b in range(2):
            both = dot(five, wl[2 * a + b])
            for x in range(2):
                for y in range(2):
                    at = 24 * (2 * x + y)
                    for cz in range(2):
                        zs = pl.ds(cz, 24, stride=2)
                        s6[2 * x + a, 2 * y + b, zs, :] = (
                            f6[2 * x + a, 2 * y + b, zs, :]
                            + both[at : at + 24, 128 * cz : 128 * cz + 128]
                        )
    out[...] = s6[:, :, :, 0:C]

    for n in range(3):
        mate_copy(n).wait_send()
        share_copy(n).wait_send()
    each(five_copy, 1, sends_to, lambda copy: copy.wait_send())
    each(rim_copy, 1, sends_to, lambda copy: copy.wait_send())
    each(four_copy, 2, sends_to, lambda copy: copy.wait_send())
    over_partners(lambda n: three_copy(n).wait_send())


def local(leaf_multipoles, occupancy, m2m_ops, m2l_ops, l2l_ops):
    leaf = jnp.transpose(leaf_multipoles, (1, 2, 3, 0))
    m2m = jnp.transpose(m2m_ops, (0, 1, 3, 2, 4)).reshape(8 * C, C)
    l2l = jnp.transpose(l2l_ops, (0, 1, 3, 2, 4)).reshape(8 * C, C)
    vmem = pl.BlockSpec(memory_space=pltpu.VMEM)
    dma = pltpu.SemaphoreType.DMA
    result = pl.pallas_call(
        kernel,
        out_shape=jax.ShapeDtypeStruct((4, 4, 48, C), F32),
        in_specs=[vmem] * 4 + [pl.BlockSpec(memory_space=pl.ANY)],
        out_specs=vmem,
        scratch_shapes=[
            pltpu.VMEM((7, 7, 7, C, C), BF16),
            pltpu.VMEM((7, 7, 7, 128, 128), BF16),
            pltpu.VMEM((984, 128), F32),
            pltpu.VMEM((4, 256, 128), BF16),
            pltpu.VMEM((984, 128), F32),
            pltpu.VMEM((4, 128, 256), BF16),
            pltpu.VMEM((4, 4, 48, 128), F32),
            pltpu.VMEM((4, 8, 48, 256), BF16),
            pltpu.VMEM((2, 64, 128), F32),
            pltpu.VMEM((3, 3, 48, 256), BF16),
            pltpu.VMEM((3, 3, 2, 2, 16, 128), BF16),
            pltpu.VMEM((2, 2, 16, 128), F32),
            pltpu.VMEM((16, 128), BF16),
            pltpu.VMEM((2, 2, 4, 4, 16, 128), BF16),
            pltpu.VMEM((2, 2, 256, 128), F32),
            pltpu.VMEM((4, 4, 8, 128), F32),
            pltpu.VMEM((2, 48, 128), F32),
            pltpu.VMEM((4, 2, 48, 128), F32),
            pltpu.VMEM((3, 8, 10, 16, 256), BF16),
            pltpu.VMEM((3, 7, 10, 16, 256), BF16),
            pltpu.VMEM((4, 6, 16, 256), F32),
            pltpu.VMEM((6, 16, 256), F32),
            pltpu.VMEM((4, 4, 48, 128), F32),
            pltpu.VMEM((2, 2, 48, 128), F32),
            pltpu.VMEM((7, 32, 128), F32),
            dma((7,)),
            dma((8,)),
            dma((8,)),
            dma((8,)),
            dma((8,)),
            dma((3,)),
            dma((3,)),
            dma((8,)),
            dma((8,)),
            dma((16,)),
            dma((16,)),
            dma((3,)),
            dma((3,)),
        ],
        compiler_params=pltpu.CompilerParams(
            collective_id=0, has_side_effects=True, vmem_limit_bytes=56 * 2**20
        ),
    )(leaf, occupancy, m2m, l2l, m2l_ops)
    return jnp.transpose(result, (3, 0, 1, 2))


def solution(mesh):
    placed = (P(None, "row", "col", None), P("row", "col", None), P(), P(), P())
    return jax.shard_map(
        local, mesh=mesh, in_specs=placed, out_specs=P(None, "row", "col", None), check_vma=False
    )
```
